32 devices in a mesh: row: 8 (over z, x), col: 4 (over y, core).
Axes of the slice: x: 2, y: 2, z: 4, core: 2. Of those that a mesh axis runs over, the one named last changes fastest.
Arguments:
- elemental: bfloat16 [2, 512, 512, 512], P(None, 'row', 'col'), may hold values from -6 to 6
- perambulators: bfloat16 [32, 2, 512, 512], P(('row', 'col')), may hold values from -0.1875 to 0.1875
- source_owner: int32 [1], replicated, may hold values from 0 to 31
Outputs:
- contracted: float32 [2, 512, 512, 512], P(None, None, 'row', 'col')
The draws below stay inside these ranges and needn't reach their ends.
All inputs are finite; a program needn't handle non-finite values.
Results may differ from the reference program's by a relative error of at most 0.0041.
Values may be sent and summed in bfloat16 or wider, within the bound.
No kernel may reach another device: no remote copies, remote signals or barrier semaphores. Data moves between devices by JAX's collectives and lax.ppermute only.
A program may use at most 128 MiB of HBM per device.

```python
import jax
import jax.numpy as jnp

N = 512
SOURCES = 32


def shard_levels(key, dims, split, smallest, largest):
    loudness, own = 1.0, jax.random.fold_in(key, 6)
    for dim, shards_of in split:
        steps = jnp.exp(jax.random.uniform(jax.random.fold_in(own, dim), (shards_of,), jnp.float32, smallest / len(split), largest / len(split)))
        loudness = loudness * jnp.repeat(steps, dims[dim] // shards_of).reshape([-1 if axis == dim else 1 for axis in range(len(dims))])
    return loudness


def gaussian(rng, shape, scale, reach, shards=(), kind=jnp.bfloat16):
    drawn = jax.random.normal(rng, shape, jnp.float32) * scale
    if len(shards) > 0:
        drawn = shard_levels(rng, shape, shards, -0.22, 0.18) * drawn
    return jnp.clip(drawn, min=-reach, max=reach).astype(kind)


def setup_inputs(seed: int = 0) -> dict:
    streams_of = jax.random.split(jax.random.key(seed), 4)
    elemental = gaussian(streams_of[0], (2, N, N, N), 1.0, 6.0, ((1, 8), (2, 4)))
    perambulators = gaussian(streams_of[1], (SOURCES, 2, N, N), (2 * N) ** -0.5, 0.1875, ((0, 32),))
    source_owner = jax.random.randint(streams_of[2], (1,), 0, SOURCES).astype(jnp.int32)
    return {"elemental": elemental, "perambulators": perambulators, "source_owner": source_owner}


def build_mixing(peramb):
    real_part = peramb[0]
    imag_part = peramb[1]
    upper = jnp.concatenate([real_part, -imag_part], axis=1)
    lower = jnp.concatenate([imag_part, real_part], axis=1)
    full = jnp.concatenate([upper, lower], axis=0)
    return full.reshape(2, N, 2, N)


def reference(elemental, perambulators, source_owner):
    chosen = perambulators[source_owner[0]]
    mixing = build_mixing(chosen).astype(jnp.float32)
    first = jnp.einsum("scrk,rijk->sijc", mixing, elemental.astype(jnp.float32))
    first = first.astype(jnp.bfloat16).astype(jnp.float32)
    second = jnp.einsum("sbrj,rijc->sbic", mixing, first)
    second = second.astype(jnp.bfloat16).astype(jnp.float32)
    return jnp.einsum("sari,rbic->sabc", mixing, second)
```

```python
import functools

import jax
import jax.numpy as jnp
from jax import lax
from jax.experimental import pallas as pl
from jax.experimental.pallas import tpu as pltpu
from jax.sharding import PartitionSpec as P

VMEM_BYTES = 56 * 1024 * 1024


def is_power_of_two(n):
    return n & (n - 1) == 0


def flip(n, bit):
    return [(i, i ^ bit) for i in range(n)]


def take_from_owner(block, axis, bit, owner):
    received = lax.ppermute(block, axis, flip(lax.axis_size(axis), bit))
    return jnp.where((lax.axis_index(axis) & bit) == (owner & bit), block, received)


def broadcast_rows(block, owner_row, owner_col):
    row_count, col_count = lax.axis_size("row"), lax.axis_size("col")
    if not (is_power_of_two(row_count) and is_power_of_two(col_count)):
        mine = (lax.axis_index("row") == owner_row) & (lax.axis_index("col") == owner_col)
        return lax.psum(jnp.where(mine, block, jnp.zeros_like(block)), ("row", "col"))
    steps = [("row", 1 << n, owner_row) for n in range(row_count.bit_length() - 1)]
    steps += [("col", 1 << n, owner_col) for n in range(1, col_count.bit_length() - 1)]
    paired = col_count > 1
    whole = block
    if paired:
        whole = take_from_owner(block, "col", 1, owner_col)
        half = block.shape[0] // 2
        low = (lax.axis_index("col") & 1) == 0
        block = jnp.where(low, whole[:half], whole[half:])
    pieces = 3
    rows = block.shape[0]
    cuts = [rows * p // pieces // 16 * 16 for p in range(pieces)] + [rows]
    parts = [block[cuts[p] : cuts[p + 1]] for p in range(pieces)]
    for n in range(len(steps)):
        for p in range(pieces):
            axis, bit, owner = steps[(n + p) % len(steps)]
            parts[p] = take_from_owner(parts[p], axis, bit, owner)
    block = jnp.concatenate(parts)
    if paired:
        other = lax.ppermute(block, "col", flip(col_count, 1))
        block = jnp.concatenate([jnp.where(low, block, other), jnp.where(low, other, block)])
    return block


def first_kernel(place, mixing, elem, *outs):
    width = elem.shape[-1]
    count, local_j = elem.shape[1], elem.shape[2]
    cols = outs[0].shape[-1]
    left = jnp.concatenate(
        [elem[0].reshape(count * local_j, width), elem[1].reshape(count * local_j, width)], axis=1
    )
    for t, out in enumerate(outs):
        start = pl.multiple_of((place[1] ^ t) * cols, cols)
        right = jnp.concatenate(
            [mixing[pl.ds(start, cols), :], mixing[pl.ds(width + start, cols), :]], axis=0
        )
        res = lax.dot_general(
            left, right, (((1,), (1,)), ((), ())), preferred_element_type=jnp.float32
        ).astype(jnp.bfloat16)
        for s in range(2):
            out[s] = res[:, s * cols : (s + 1) * cols].reshape(count, local_j, cols)


def contract_first(mixing, elemental, place, offset, count, col_count):
    _, _, local_j, width = elemental.shape
    cols = width // col_count
    step = count if offset == 0 else min(offset, count)
    while count % step or offset % step or step > 4:
        step -= 1
    out_shape = jax.ShapeDtypeStruct((2, count, local_j, cols), jnp.bfloat16)
    return pl.pallas_call(
        first_kernel,
        name="first",
        grid=(count // step,),
        in_specs=[
            pl.BlockSpec(memory_space=pltpu.SMEM),
            pl.BlockSpec(mixing.shape, lambda n: (0, 0)),
            pl.BlockSpec((2, step, local_j, width), lambda n: (0, offset // step + n, 0, 0)),
        ],
        out_specs=[pl.BlockSpec((2, step, local_j, cols), lambda n: (0, n, 0, 0))] * col_count,
        out_shape=[out_shape] * col_count,
        compiler_params=pltpu.CompilerParams(vmem_limit_bytes=VMEM_BYTES),
        cost_estimate=pl.CostEstimate(
            flops=8 * count * local_j * width * width,
            bytes_accessed=8 * count * local_j * width + 8 * width * width,
            transcendentals=0,
        ),
    )(place, mixing, elemental)


def second_kernel(col_count, row_count, splits, place, mixing, *refs):
    blocks, outs, (ordered, right) = refs[:col_count], refs[col_count:-2], refs[-2:]
    width = mixing.shape[0] // 2
    _, count, local_j, cols = blocks[0].shape
    local_b = width // row_count

    @pl.when(pl.program_id(0) == 0)
    def _():
        for t in range(row_count):
            start = pl.multiple_of((place[0] ^ t) * local_b, local_b)
            for s in range(2):
                ordered[pl.ds((2 * t + s) * local_b, local_b), :] = mixing[
                    pl.ds(s * width + start, local_b), :
                ]

    for t, block in enumerate(blocks):
        start = pl.multiple_of((place[1] ^ t) * local_j, local_j)
        for r in range(2):
            for i in range(count):
                right[pl.ds(r * width + start, local_j), i * cols : (i + 1) * cols] = block[r, i]
    res = jnp.dot(ordered[...], right[...], preferred_element_type=jnp.float32)
    res = res.astype(jnp.bfloat16)
    part = local_b // splits
    for u in range(splits):
        for t in range(row_count):
            for s in range(2):
                row = (2 * t + s) * local_b + u * part
                for i in range(count):
                    outs[u * row_count + t][s, i] = res[
                        row : row + part, i * cols : (i + 1) * cols
                    ]


def contract_second(mixing, blocks, place, row_count, splits):
    col_count = len(blocks)
    _, count, local_j, cols = blocks[0].shape
    width = mixing.shape[0] // 2
    part = width // row_count // splits
    step = min(count, 4)
    while count % step:
        step -= 1
    out_shape = jax.ShapeDtypeStruct((2, count, part, cols), jnp.bfloat16)
    outs = pl.pallas_call(
        functools.partial(second_kernel, col_count, row_count, splits),
        name="second",
        grid=(count // step,),
        in_specs=[
            pl.BlockSpec(memory_space=pltpu.SMEM),
            pl.BlockSpec(mixing.shape, lambda n: (0, 0)),
        ]
        + [pl.BlockSpec((2, step, local_j, cols), lambda n: (0, n, 0, 0))] * col_count,
        out_specs=[pl.BlockSpec((2, step, part, cols), lambda n: (0, n, 0, 0))]
        * (row_count * splits),
        out_shape=[out_shape] * (row_count * splits),
        scratch_shapes=[
            pltpu.VMEM(mixing.shape, jnp.bfloat16),
            pltpu.VMEM((2 * width, step * cols), jnp.bfloat16),
        ],
        compiler_params=pltpu.CompilerParams(vmem_limit_bytes=VMEM_BYTES),
        cost_estimate=pl.CostEstimate(
            flops=8 * count * cols * width * width,
            bytes_accessed=8 * count * cols * width + 8 * width * width,
            transcendentals=0,
        ),
    )(place, mixing, *blocks)
    return [outs[u * row_count : (u + 1) * row_count] for u in range(splits)]


def third_kernel(row_count, offsets, rows, aliased, place, mixing, *refs):
    total = row_count * len(offsets)
    blocks, (out, gathered) = refs[:total], refs[total + aliased :]
    width = mixing.shape[0] // 2
    local_i = width // row_count
    depth, part, cols = gathered.shape

    @pl.when(pl.program_id(0) == 0)
    def _():
        for n, block in enumerate(blocks):
            chunk, t = divmod(n, row_count)
            source = place[0] ^ t
            for r in range(2):
                start = r * width + source * local_i + offsets[chunk]
                gathered[pl.ds(start, block.shape[1])] = block[r].astype(jnp.float32)

    flat = gathered.reshape(depth * part, cols)
    result = out.reshape(depth * rows, cols)
    base = pl.program_id(0) * rows
    for b in range(0, rows, 2):
        right = jnp.concatenate(
            [
                flat[pl.ds(base + b + n, depth, stride=part), :].astype(jnp.bfloat16)
                for n in range(2)
            ],
            axis=1,
        )
        res = jnp.dot(mixing[...], right, preferred_element_type=jnp.float32)
        for n in range(2):
            result[pl.ds(b + n, depth, stride=rows), :] = res[:, n * cols : (n + 1) * cols]


def contract_third(mixing, chunks, place, offsets, index, splits, previous):
    row_count = len(chunks[0])
    depth = mixing.shape[0]
    cols = chunks[0][0].shape[-1]
    part = chunks[-1][0].shape[2]
    rows = 8
    in_specs = [
        pl.BlockSpec(memory_space=pltpu.SMEM),
        pl.BlockSpec(mixing.shape, lambda n: (0, 0)),
    ]
    operands = [place, mixing]
    for q, chunk in enumerate(chunks):
        where = index if chunk[0].shape[2] != part else 0
        for block in chunk:
            shape = (2, block.shape[1], part, cols)
            in_specs.append(pl.BlockSpec(shape, lambda n, where=where: (0, 0, where, 0)))
            operands.append(block)
    aliases = {}
    if previous is not None:
        aliases = {len(operands): 0}
        in_specs.append(pl.BlockSpec(memory_space=pl.ANY))
        operands.append(previous)
    return pl.pallas_call(
        functools.partial(third_kernel, row_count, offsets, rows, len(aliases)),
        name="third",
        grid=(part // rows,),
        in_specs=in_specs,
        out_specs=pl.BlockSpec((depth, rows, cols), lambda n: (0, index * (part // rows) + n, 0)),
        out_shape=jax.ShapeDtypeStruct((depth, part * splits, cols), jnp.float32),
        scratch_shapes=[pltpu.VMEM((depth, part, cols), jnp.float32)],
        input_output_aliases=aliases,
        compiler_params=pltpu.CompilerParams(vmem_limit_bytes=VMEM_BYTES),
        cost_estimate=pl.CostEstimate(
            flops=2 * depth * depth * part * cols,
            bytes_accessed=6 * depth * part * cols + 2 * depth * depth,
            transcendentals=0,
        ),
    )(*operands)


def build_mixing(peramb):
    real_part, imag_part = peramb
    upper = jnp.concatenate([real_part, -imag_part], axis=1)
    lower = jnp.concatenate([imag_part, real_part], axis=1)
    return jnp.concatenate([upper, lower], axis=0)


class Lane:
    def __init__(self, axis, depth):
        self.axis = axis
        self.depth = depth
        self.results = []

    def send(self, block, bit):
        if len(self.results) >= self.depth:
            block, _ = lax.optimization_barrier((block, self.results[-self.depth]))
        result = lax.ppermute(block, self.axis, flip(lax.axis_size(self.axis), bit))
        self.results.append(result)
        return result


def after(value, *others):
    if not others:
        return value
    return lax.optimization_barrier((value, others))[0]


def per_device(elemental, perambulators, source_owner):
    owner = source_owner[0]
    row_count, col_count = lax.axis_size("row"), lax.axis_size("col")
    place = jnp.stack([lax.axis_index("row"), lax.axis_index("col")]).astype(jnp.int32)
    _, local_i, local_j, width = elemental.shape
    local_b, cols = width // row_count, width // col_count
    chosen = broadcast_rows(
        perambulators[0].reshape(2 * width, width), owner // col_count, owner % col_count
    )
    mixing = build_mixing(chosen.reshape(2, width, width))

    if cols % 128 or local_b % 16 or local_i % 16 or not is_power_of_two(row_count * col_count):
        mixing = mixing.reshape(2, width, 2, width)
        first = jnp.einsum("scrk,rijk->sijc", mixing, elemental, preferred_element_type=jnp.float32)
        first = lax.all_to_all(first.astype(jnp.bfloat16), "col", 3, 2, tiled=True)
        second = jnp.einsum("sbrj,rijc->sbic", mixing, first, preferred_element_type=jnp.float32)
        second = lax.all_to_all(second.astype(jnp.bfloat16), "row", 1, 2, tiled=True)
        return jnp.einsum("sari,rbic->sabc", mixing, second, preferred_element_type=jnp.float32)

    counts = [local_i // 16, local_i // 8, local_i * 5 // 16]
    counts.append(local_i - sum(counts))
    offsets = [sum(counts[:q]) for q in range(len(counts))]
    splits = local_b // 16
    half = row_count // 2
    order = [half] + [t for n in range(1, half) for t in (n, half + n)]
    col_lane, row_lane = Lane("col", 2), Lane("row", 3)
    last = len(counts) - 1
    firsts, chunks, tails = {}, [], []

    def start(q, token, wait):
        blocks = contract_first(mixing, elemental, after(place, token), offsets[q], counts[q], col_count)
        blocks = after(blocks, *wait)
        firsts[q] = [blocks[0]] + [col_lane.send(blocks[t], t) for t in range(1, col_count)]

    start(0, mixing, [])
    start(1, mixing, [])
    for q in range(len(counts)):
        parts = contract_second(
            mixing, firsts[q], place, row_count, splits if q == last else 1
        )
        for part in parts:
            arrived = {0: part[0]}
            for t in order:
                arrived[t] = row_lane.send(part[t], t)
            (tails if q == last else chunks).append([arrived[t] for t in range(row_count)])
        if q + 2 <= last:
            start(q + 2, parts[0][0], [arrived[t] for t in order])
    result = None
    for u, tail in enumerate(tails):
        result = contract_third(mixing, chunks + [tail], place, offsets, u, splits, result)
    return result.reshape(2, width, local_b, cols)


def solution(mesh):
    in_specs = (P(None, "row", "col", None), P(("row", "col"), None, None, None), P())
    out_specs = P(None, None, "row", "col")
    return jax.shard_map(
        per_device, mesh=mesh, in_specs=in_specs, out_specs=out_specs, check_vma=False
    )
```

```python
import functools

import jax
import jax.numpy as jnp
from jax import lax
from jax.experimental import pallas as pl
from jax.experimental.pallas import tpu as pltpu
from jax.sharding import PartitionSpec as P

COUNTS = (3, 5, 8, 16)
DEPTH = 5
WAIT = 3
FIRST = 5
SECOND = 6
BLOCK = 16
VMEM_BYTES = 56 * 1024 * 1024


def is_power_of_two(n):
    return n & (n - 1) == 0


def flip(n, bit):
    return [(i, i ^ bit) for i in range(n)]


def take_from_owner(block, axis, bit, owner):
    received = lax.ppermute(block, axis, flip(lax.axis_size(axis), bit))
    return jnp.where((lax.axis_index(axis) & bit) == (owner & bit), block, received)


def broadcast_rows(block, owner_row, owner_col):
    row_count, col_count = lax.axis_size("row"), lax.axis_size("col")
    if not (is_power_of_two(row_count) and is_power_of_two(col_count)):
        mine = (lax.axis_index("row") == owner_row) & (lax.axis_index("col") == owner_col)
        return lax.psum(jnp.where(mine, block, jnp.zeros_like(block)), ("row", "col"))
    steps = [("row", 1 << n, owner_row) for n in range(row_count.bit_length() - 1)]
    steps += [("col", 1 << n, owner_col) for n in range(1, col_count.bit_length() - 1)]
    paired = col_count > 1
    whole = block
    if paired:
        whole = take_from_owner(block, "col", 1, owner_col)
        half = block.shape[0] // 2
        low = (lax.axis_index("col") & 1) == 0
        block = jnp.where(low, whole[:half], whole[half:])
    pieces = 3
    rows = block.shape[0]
    cuts = [rows * p // pieces // 16 * 16 for p in range(pieces)] + [rows]
    parts = [block[cuts[p] : cuts[p + 1]] for p in range(pieces)]
    for n in range(len(steps)):
        for p in range(pieces):
            axis, bit, owner = steps[(n + p) % len(steps)]
            parts[p] = take_from_owner(parts[p], axis, bit, owner)
    block = jnp.concatenate(parts)
    if paired:
        other = lax.ppermute(block, "col", flip(col_count, 1))
        block = jnp.concatenate([jnp.where(low, block, other), jnp.where(low, other, block)])
    return block


def first_kernel(mixing, elem, out):
    width = elem.shape[-1]
    count, local_j = elem.shape[1], elem.shape[2]
    cols = out.shape[-1]
    left = jnp.concatenate(
        [elem[0].reshape(count * local_j, width), elem[1].reshape(count * local_j, width)], axis=1
    )
    for d in range(out.shape[0]):
        right = jnp.concatenate(
            [mixing[s * width + d * cols : s * width + (d + 1) * cols, :] for s in range(2)], axis=0
        )
        res = lax.dot_general(
            left, right, (((1,), (1,)), ((), ())), preferred_element_type=jnp.float32
        ).astype(jnp.bfloat16)
        for s in range(2):
            out[d, s] = res[:, s * cols : (s + 1) * cols].reshape(count, local_j, cols)


def contract_first(mixing, elemental, offset, count, col_count):
    _, _, local_j, width = elemental.shape
    cols = width // col_count
    step = count if offset == 0 else min(offset, count)
    while count % step or offset % step or step > 4:
        step -= 1
    return pl.pallas_call(
        first_kernel,
        name="first",
        grid=(count // step,),
        in_specs=[
            pl.BlockSpec(mixing.shape, lambda n: (0, 0)),
            pl.BlockSpec((2, step, local_j, width), lambda n: (0, offset // step + n, 0, 0)),
        ],
        out_specs=pl.BlockSpec((col_count, 2, step, local_j, cols), lambda n: (0, 0, n, 0, 0)),
        out_shape=jax.ShapeDtypeStruct((col_count, 2, count, local_j, cols), jnp.bfloat16),
        compiler_params=pltpu.CompilerParams(vmem_limit_bytes=VMEM_BYTES),
        cost_estimate=pl.CostEstimate(
            flops=8 * count * local_j * width * width,
            bytes_accessed=8 * count * local_j * width + 8 * width * width,
            transcendentals=0,
        ),
    )(mixing, elemental)


def gathered_kernel(place, mixing, elem, out):
    width, cols = mixing.shape[0] // 2, out.shape[-1]
    col_count, _, count, local_j, _ = elem.shape
    start = pl.multiple_of(place[1] * cols, cols)
    right = jnp.concatenate(
        [mixing[pl.ds(start, cols), :], mixing[pl.ds(width + start, cols), :]], axis=0
    )
    for d in range(col_count):
        left = jnp.concatenate(
            [elem[d, r].reshape(count * local_j, width) for r in range(2)], axis=1
        )
        res = lax.dot_general(
            left, right, (((1,), (1,)), ((), ())), preferred_element_type=jnp.float32
        ).astype(jnp.bfloat16)
        for s in range(2):
            out[d, s] = res[:, s * cols : (s + 1) * cols].reshape(count, local_j, cols)


def contract_gathered(mixing, gathered, place):
    col_count, _, count, local_j, width = gathered.shape
    cols = width // col_count
    step = 2 if count % 2 == 0 else 1
    return pl.pallas_call(
        gathered_kernel,
        name="gathered",
        grid=(count // step,),
        in_specs=[
            pl.BlockSpec(memory_space=pltpu.SMEM),
            pl.BlockSpec(mixing.shape, lambda n: (0, 0)),
            pl.BlockSpec((col_count, 2, step, local_j, width), lambda n: (0, 0, n, 0, 0)),
        ],
        out_specs=pl.BlockSpec((col_count, 2, step, local_j, cols), lambda n: (0, 0, n, 0, 0)),
        out_shape=jax.ShapeDtypeStruct((col_count, 2, count, local_j, cols), jnp.bfloat16),
        compiler_params=pltpu.CompilerParams(vmem_limit_bytes=VMEM_BYTES),
        cost_estimate=pl.CostEstimate(
            flops=8 * count * local_j * width * width,
            bytes_accessed=8 * count * local_j * width + 8 * width * width,
            transcendentals=0,
        ),
    )(place, mixing, gathered)


def second_kernel(row_count, parts, place, mixing, block, *refs):
    outs, (ordered, right) = refs[:-2], refs[-2:]
    width = mixing.shape[0] // 2
    col_count, _, count, local_j, cols = block.shape
    local_b = width // row_count

    @pl.when(pl.program_id(0) == 0)
    def _():
        for t in range(row_count):
            start = pl.multiple_of((place[0] ^ t) * local_b, local_b)
            for s in range(2):
                ordered[pl.ds((2 * t + s) * local_b, local_b), :] = mixing[
                    pl.ds(s * width + start, local_b), :
                ]

    for d in range(col_count):
        for r in range(2):
            row = r * width + d * local_j
            for i in range(count):
                right[row : row + local_j, i * cols : (i + 1) * cols] = block[d, r, i]
    res = jnp.dot(ordered[...], right[...], preferred_element_type=jnp.float32)
    res = res.astype(jnp.bfloat16)
    for u, part in enumerate(parts):
        for t in range(row_count):
            for s in range(2):
                row = (2 * t + s) * local_b + sum(parts[:u])
                for i in range(count):
                    outs[u * row_count + t][s, i] = res[
                        row : row + part, i * cols : (i + 1) * cols
                    ]


def contract_second(mixing, block, place, row_count, parts):
    col_count, _, count, local_j, cols = block.shape
    width = mixing.shape[0] // 2
    step = min(count, 4)
    while count % step:
        step -= 1
    shapes = [(2, count, part, cols) for part in parts for _ in range(row_count)]
    outs = pl.pallas_call(
        functools.partial(second_kernel, row_count, parts),
        name="second",
        grid=(count // step,),
        in_specs=[
            pl.BlockSpec(memory_space=pltpu.SMEM),
            pl.BlockSpec(mixing.shape, lambda n: (0, 0)),
        ]
        + [pl.BlockSpec((col_count, 2, step, local_j, cols), lambda n: (0, 0, n, 0, 0))],
        out_specs=[
            pl.BlockSpec((2, step) + shape[2:], lambda n: (0, n, 0, 0)) for shape in shapes
        ],
        out_shape=[jax.ShapeDtypeStruct(shape, jnp.bfloat16) for shape in shapes],
        scratch_shapes=[
            pltpu.VMEM(mixing.shape, jnp.bfloat16),
            pltpu.VMEM((2 * width, step * cols), jnp.bfloat16),
        ],
        compiler_params=pltpu.CompilerParams(vmem_limit_bytes=VMEM_BYTES),
        cost_estimate=pl.CostEstimate(
            flops=8 * count * cols * width * width,
            bytes_accessed=8 * count * cols * width + 8 * width * width,
            transcendentals=0,
        ),
    )(place, mixing, block)
    return [outs[u * row_count : (u + 1) * row_count] for u in range(len(parts))]


def third_kernel(row_count, offsets, rows, aliased, place, mixing, *refs):
    total = row_count * len(offsets)
    blocks, (out, gathered) = refs[:total], refs[total + aliased :]
    width = mixing.shape[0] // 2
    local_i = width // row_count
    depth, part, cols = gathered.shape

    @pl.when(pl.program_id(0) == 0)
    def _():
        for n, block in enumerate(blocks):
            chunk, t = divmod(n, row_count)
            source = place[0] ^ t
            for r in range(2):
                start = r * width + source * local_i + offsets[chunk]
                gathered[pl.ds(start, block.shape[1])] = block[r].astype(jnp.float32)

    flat = gathered.reshape(depth * part, cols)
    result = out.reshape(depth * rows, cols)
    base = pl.program_id(0) * rows
    for b in range(0, rows, 2):
        right = jnp.concatenate(
            [
                flat[pl.ds(base + b + n, depth, stride=part), :].astype(jnp.bfloat16)
                for n in range(2)
            ],
            axis=1,
        )
        res = jnp.dot(mixing[...], right, preferred_element_type=jnp.float32)
        for n in range(2):
            result[pl.ds(b + n, depth, stride=rows), :] = res[:, n * cols : (n + 1) * cols]


def contract_third(mixing, chunks, places, place, offsets, index, local_b, previous):
    row_count = len(chunks[0])
    depth, cols = mixing.shape[0], chunks[0][0].shape[-1]
    part, rows = BLOCK, 8
    in_specs = [
        pl.BlockSpec(memory_space=pltpu.SMEM),
        pl.BlockSpec(mixing.shape, lambda n: (0, 0)),
    ]
    operands = [place, mixing]
    for chunk, where in zip(chunks, places):
        for block in chunk:
            shape = (2, block.shape[1], part, cols)
            in_specs.append(pl.BlockSpec(shape, lambda n, where=where: (0, 0, where, 0)))
            operands.append(block)
    aliases = {}
    if previous is not None:
        aliases = {len(operands): 0}
        in_specs.append(pl.BlockSpec(memory_space=pl.ANY))
        operands.append(previous)
    return pl.pallas_call(
        functools.partial(third_kernel, row_count, offsets, rows, len(aliases)),
        name="third",
        grid=(part // rows,),
        in_specs=in_specs,
        out_specs=pl.BlockSpec((depth, rows, cols), lambda n: (0, index * (part // rows) + n, 0)),
        out_shape=jax.ShapeDtypeStruct((depth, local_b, cols), jnp.float32),
        scratch_shapes=[pltpu.VMEM((depth, part, cols), jnp.float32)],
        input_output_aliases=aliases,
        compiler_params=pltpu.CompilerParams(vmem_limit_bytes=VMEM_BYTES),
        cost_estimate=pl.CostEstimate(
            flops=2 * depth * depth * part * cols,
            bytes_accessed=6 * depth * part * cols + 2 * depth * depth,
            transcendentals=0,
        ),
    )(*operands)


def build_mixing(peramb):
    real_part, imag_part = peramb
    upper = jnp.concatenate([real_part, -imag_part], axis=1)
    lower = jnp.concatenate([imag_part, real_part], axis=1)
    return jnp.concatenate([upper, lower], axis=0)


class Lane:
    def __init__(self, axis, depth):
        self.axis = axis
        self.depth = depth
        self.results = []

    def send(self, block, bit, *others):
        before = self.results[-self.depth :][: len(self.results) >= self.depth]
        block = after(block, *before, *others)
        result = lax.ppermute(block, self.axis, flip(lax.axis_size(self.axis), bit))
        self.results.append(result)
        return result


def after(value, *others):
    if not others:
        return value
    return lax.optimization_barrier((value, others))[0]


def per_device(elemental, perambulators, source_owner):
    owner = source_owner[0]
    row_count, col_count = lax.axis_size("row"), lax.axis_size("col")
    place = jnp.stack([lax.axis_index("row"), lax.axis_index("col")]).astype(jnp.int32)
    _, local_i, local_j, width = elemental.shape
    local_b, cols = width // row_count, width // col_count
    chosen = broadcast_rows(
        perambulators[0].reshape(2 * width, width), owner // col_count, owner % col_count
    )
    mixing = build_mixing(chosen.reshape(2, width, width))

    if cols % 128 or local_b % BLOCK or local_i % 16 or not is_power_of_two(row_count * col_count):
        mixing = mixing.reshape(2, width, 2, width)
        first = jnp.einsum("scrk,rijk->sijc", mixing, elemental, preferred_element_type=jnp.float32)
        first = lax.all_to_all(first.astype(jnp.bfloat16), "col", 3, 2, tiled=True)
        second = jnp.einsum("sbrj,rijc->sbic", mixing, first, preferred_element_type=jnp.float32)
        second = lax.all_to_all(second.astype(jnp.bfloat16), "row", 1, 2, tiled=True)
        return jnp.einsum("sari,rbic->sabc", mixing, second, preferred_element_type=jnp.float32)

    counts = [local_i * n // sum(COUNTS) for n in COUNTS[:-1]]
    counts.append(local_i - sum(counts))
    offsets = [sum(counts[:q]) for q in range(len(counts))]
    half = row_count // 2
    order = [half] + [t for n in range(1, half) for t in (n, half + n)]
    order[-2:] = order[:-3:-1]
    row_lane = Lane("row", DEPTH)
    last = len(counts) - 1
    tail = [BLOCK] * (local_b // BLOCK)
    chunks, tails = [], []

    def contract(q, *others):
        return contract_first(
            mixing, after(elemental, *others), offsets[q], counts[q], col_count
        )

    def send_first(block, *others):
        return lax.all_to_all(after(block, *others), "col", 0, 0, tiled=True)

    def send_second(part, waits):
        arrived = {0: part[0]}
        for n, t in enumerate(order):
            arrived[t] = row_lane.send(part[t], t, *waits.get(n, []))
        return [arrived[t] for t in range(row_count)]

    raw = lax.all_gather(elemental[:, : counts[0]], "col")
    following = contract(1)
    swapped = contract_gathered(mixing, raw, after(place, following))
    parts = contract_second(mixing, swapped, place, row_count, [local_b])
    swapped = send_first(following, swapped)
    for q in range(last):
        waits = {}
        if q + 2 <= last:
            following = contract(q + 2, parts[0][0])
            waits[FIRST] = [following]
        now = parts[0]
        parts = contract_second(
            mixing, swapped, place, row_count, tail if q + 1 == last else [local_b]
        )
        waits[SECOND] = [parts[0][0]]
        chunks.append(send_second(now, waits))
        if q + 2 <= last:
            held = [chunks[q][t] for t in order[:WAIT]]
            swapped = send_first(following, swapped, *held)
    for part in parts:
        tails.append(send_second(part, {}))
    result, index = None, 0
    for part, blocks in zip(tail, tails):
        for n in range(part // BLOCK):
            result = contract_third(
                mixing, chunks + [blocks], [index] * last + [n], place, offsets, index, local_b, result
            )
            index += 1
    return result.reshape(2, width, local_b, cols)


def solution(mesh):
    in_specs = (P(None, "row", "col", None), P(("row", "col"), None, None, None), P())
    out_specs = P(None, None, "row", "col")
    return jax.shard_map(
        per_device, mesh=mesh, in_specs=in_specs, out_specs=out_specs, check_vma=False
    )
```

```python
import functools

import jax
import jax.numpy as jnp
from jax import lax
from jax.experimental import pallas as pl
from jax.experimental.pallas import tpu as pltpu
from jax.sharding import PartitionSpec as P

COUNTS = (3, 5, 8, 16)
DEPTH = 5
WAIT = 4
FIRST = 5
SECOND = 6
BLOCK = 16
VMEM_BYTES = 56 * 1024 * 1024


def is_power_of_two(n):
    return n & (n - 1) == 0


def flip(n, bit):
    return [(i, i ^ bit) for i in range(n)]


def take_from_owner(block, axis, bit, owner):
    received = lax.ppermute(block, axis, flip(lax.axis_size(axis), bit))
    return jnp.where((lax.axis_index(axis) & bit) == (owner & bit), block, received)


def broadcast_rows(block, owner_row, owner_col):
    row_count, col_count = lax.axis_size("row"), lax.axis_size("col")
    if not (is_power_of_two(row_count) and is_power_of_two(col_count)):
        mine = (lax.axis_index("row") == owner_row) & (lax.axis_index("col") == owner_col)
        return lax.psum(jnp.where(mine, block, jnp.zeros_like(block)), ("row", "col"))
    steps = [("row", 1 << n, owner_row) for n in range(row_count.bit_length() - 1)]
    steps += [("col", 1 << n, owner_col) for n in range(1, col_count.bit_length() - 1)]
    paired = col_count > 1
    whole = block
    if paired:
        whole = take_from_owner(block, "col", 1, owner_col)
        half = block.shape[0] // 2
        low = (lax.axis_index("col") & 1) == 0
        block = jnp.where(low, whole[:half], whole[half:])
    pieces = 4
    rows = block.shape[0]
    cuts = [rows * p // pieces // 16 * 16 for p in range(pieces)] + [rows]
    parts = [block[cuts[p] : cuts[p + 1]] for p in range(pieces)]
    for n in range(len(steps)):
        for p in range(pieces):
            axis, bit, owner = steps[(n + p) % len(steps)]
            parts[p] = take_from_owner(parts[p], axis, bit, owner)
    block = jnp.concatenate(parts)
    if paired:
        other = lax.ppermute(block, "col", flip(col_count, 1))
        block = jnp.concatenate([jnp.where(low, block, other), jnp.where(low, other, block)])
    return block


def first_kernel(mixing, elem, out):
    width = elem.shape[-1]
    count, local_j = elem.shape[1], elem.shape[2]
    cols = out.shape[-1]
    left = jnp.concatenate(
        [elem[0].reshape(count * local_j, width), elem[1].reshape(count * local_j, width)], axis=1
    )
    for d in range(out.shape[0]):
        right = jnp.concatenate(
            [mixing[s * width + d * cols : s * width + (d + 1) * cols, :] for s in range(2)], axis=0
        )
        res = lax.dot_general(
            left, right, (((1,), (1,)), ((), ())), preferred_element_type=jnp.float32
        ).astype(jnp.bfloat16)
        for s in range(2):
            out[d, s] = res[:, s * cols : (s + 1) * cols].reshape(count, local_j, cols)


def contract_first(mixing, elemental, offset, count, col_count):
    _, _, local_j, width = elemental.shape
    cols = width // col_count
    step = count if offset == 0 else min(offset, count)
    while count % step or offset % step or step > 4:
        step -= 1
    return pl.pallas_call(
        first_kernel,
        name="first",
        grid=(count // step,),
        in_specs=[
            pl.BlockSpec(mixing.shape, lambda n: (0, 0)),
            pl.BlockSpec((2, step, local_j, width), lambda n: (0, offset // step + n, 0, 0)),
        ],
        out_specs=pl.BlockSpec((col_count, 2, step, local_j, cols), lambda n: (0, 0, n, 0, 0)),
        out_shape=jax.ShapeDtypeStruct((col_count, 2, count, local_j, cols), jnp.bfloat16),
        compiler_params=pltpu.CompilerParams(vmem_limit_bytes=VMEM_BYTES),
        cost_estimate=pl.CostEstimate(
            flops=8 * count * local_j * width * width,
            bytes_accessed=8 * count * local_j * width + 8 * width * width,
            transcendentals=0,
        ),
    )(mixing, elemental)


def gathered_kernel(place, mixing, elem, out):
    width, cols = mixing.shape[0] // 2, out.shape[-1]
    col_count, _, count, local_j, _ = elem.shape
    start = pl.multiple_of(place[1] * cols, cols)
    right = jnp.concatenate(
        [mixing[pl.ds(start, cols), :], mixing[pl.ds(width + start, cols), :]], axis=0
    )
    for d in range(col_count):
        left = jnp.concatenate(
            [elem[d, r].reshape(count * local_j, width) for r in range(2)], axis=1
        )
        res = lax.dot_general(
            left, right, (((1,), (1,)), ((), ())), preferred_element_type=jnp.float32
        ).astype(jnp.bfloat16)
        for s in range(2):
            out[d, s] = res[:, s * cols : (s + 1) * cols].reshape(count, local_j, cols)


def contract_gathered(mixing, gathered, place):
    col_count, _, count, local_j, width = gathered.shape
    cols = width // col_count
    step = 2 if count % 2 == 0 else 1
    return pl.pallas_call(
        gathered_kernel,
        name="gathered",
        grid=(count // step,),
        in_specs=[
            pl.BlockSpec(memory_space=pltpu.SMEM),
            pl.BlockSpec(mixing.shape, lambda n: (0, 0)),
            pl.BlockSpec((col_count, 2, step, local_j, width), lambda n: (0, 0, n, 0, 0)),
        ],
        out_specs=pl.BlockSpec((col_count, 2, step, local_j, cols), lambda n: (0, 0, n, 0, 0)),
        out_shape=jax.ShapeDtypeStruct((col_count, 2, count, local_j, cols), jnp.bfloat16),
        compiler_params=pltpu.CompilerParams(vmem_limit_bytes=VMEM_BYTES),
        cost_estimate=pl.CostEstimate(
            flops=8 * count * local_j * width * width,
            bytes_accessed=8 * count * local_j * width + 8 * width * width,
            transcendentals=0,
        ),
    )(place, mixing, gathered)


def second_kernel(row_count, parts, place, mixing, block, *refs):
    outs, (ordered, right) = refs[:-2], refs[-2:]
    width = mixing.shape[0] // 2
    col_count, _, count, local_j, cols = block.shape
    local_b = width // row_count

    @pl.when(pl.program_id(0) == 0)
    def _():
        for t in range(row_count):
            start = pl.multiple_of((place[0] ^ t) * local_b, local_b)
            for s in range(2):
                ordered[pl.ds((2 * t + s) * local_b, local_b), :] = mixing[
                    pl.ds(s * width + start, local_b), :
                ]

    for d in range(col_count):
        for r in range(2):
            row = r * width + d * local_j
            for i in range(count):
                right[row : row + local_j, i * cols : (i + 1) * cols] = block[d, r, i]
    res = jnp.dot(ordered[...], right[...], preferred_element_type=jnp.float32)
    res = res.astype(jnp.bfloat16)
    for u, part in enumerate(parts):
        for t in range(row_count):
            for s in range(2):
                row = (2 * t + s) * local_b + sum(parts[:u])
                for i in range(count):
                    outs[u * row_count + t][s, i] = res[
                        row : row + part, i * cols : (i + 1) * cols
                    ]


def contract_second(mixing, block, place, row_count, parts):
    col_count, _, count, local_j, cols = block.shape
    width = mixing.shape[0] // 2
    step = min(count, 4)
    while count % step:
        step -= 1
    shapes = [(2, count, part, cols) for part in parts for _ in range(row_count)]
    outs = pl.pallas_call(
        functools.partial(second_kernel, row_count, parts),
        name="second",
        grid=(count // step,),
        in_specs=[
            pl.BlockSpec(memory_space=pltpu.SMEM),
            pl.BlockSpec(mixing.shape, lambda n: (0, 0)),
        ]
        + [pl.BlockSpec((col_count, 2, step, local_j, cols), lambda n: (0, 0, n, 0, 0))],
        out_specs=[
            pl.BlockSpec((2, step) + shape[2:], lambda n: (0, n, 0, 0)) for shape in shapes
        ],
        out_shape=[jax.ShapeDtypeStruct(shape, jnp.bfloat16) for shape in shapes],
        scratch_shapes=[
            pltpu.VMEM(mixing.shape, jnp.bfloat16),
            pltpu.VMEM((2 * width, step * cols), jnp.bfloat16),
        ],
        compiler_params=pltpu.CompilerParams(vmem_limit_bytes=VMEM_BYTES),
        cost_estimate=pl.CostEstimate(
            flops=8 * count * cols * width * width,
            bytes_accessed=8 * count * cols * width + 8 * width * width,
            transcendentals=0,
        ),
    )(place, mixing, block)
    return [outs[u * row_count : (u + 1) * row_count] for u in range(len(parts))]


def third_kernel(row_count, offsets, rows, aliased, place, mixing, *refs):
    total = row_count * len(offsets)
    blocks, (out, gathered) = refs[:total], refs[total + aliased :]
    width = mixing.shape[0] // 2
    local_i = width // row_count
    depth, part, cols = gathered.shape

    @pl.when(pl.program_id(0) == 0)
    def _():
        for n, block in enumerate(blocks):
            chunk, t = divmod(n, row_count)
            source = place[0] ^ t
            for r in range(2):
                start = r * width + source * local_i + offsets[chunk]
                gathered[pl.ds(start, block.shape[1])] = block[r].astype(jnp.float32)

    flat = gathered.reshape(depth * part, cols)
    result = out.reshape(depth * rows, cols)
    base = pl.program_id(0) * rows
    for b in range(0, rows, 2):
        right = jnp.concatenate(
            [
                flat[pl.ds(base + b + n, depth, stride=part), :].astype(jnp.bfloat16)
                for n in range(2)
            ],
            axis=1,
        )
        res = jnp.dot(mixing[...], right, preferred_element_type=jnp.float32)
        for n in range(2):
            result[pl.ds(b + n, depth, stride=rows), :] = res[:, n * cols : (n + 1) * cols]


def contract_third(mixing, chunks, places, place, offsets, index, local_b, previous):
    row_count = len(chunks[0])
    depth, cols = mixing.shape[0], chunks[0][0].shape[-1]
    part, rows = BLOCK, 8
    in_specs = [
        pl.BlockSpec(memory_space=pltpu.SMEM),
        pl.BlockSpec(mixing.shape, lambda n: (0, 0)),
    ]
    operands = [place, mixing]
    for chunk, where in zip(chunks, places):
        for block in chunk:
            shape = (2, block.shape[1], part, cols)
            in_specs.append(pl.BlockSpec(shape, lambda n, where=where: (0, 0, where, 0)))
            operands.append(block)
    aliases = {}
    if previous is not None:
        aliases = {len(operands): 0}
        in_specs.append(pl.BlockSpec(memory_space=pl.ANY))
        operands.append(previous)
    return pl.pallas_call(
        functools.partial(third_kernel, row_count, offsets, rows, len(aliases)),
        name="third",
        grid=(part // rows,),
        in_specs=in_specs,
        out_specs=pl.BlockSpec((depth, rows, cols), lambda n: (0, index * (part // rows) + n, 0)),
        out_shape=jax.ShapeDtypeStruct((depth, local_b, cols), jnp.float32),
        scratch_shapes=[pltpu.VMEM((depth, part, cols), jnp.float32)],
        input_output_aliases=aliases,
        compiler_params=pltpu.CompilerParams(vmem_limit_bytes=VMEM_BYTES),
        cost_estimate=pl.CostEstimate(
            flops=2 * depth * depth * part * cols,
            bytes_accessed=6 * depth * part * cols + 2 * depth * depth,
            transcendentals=0,
        ),
    )(*operands)


def build_mixing(peramb):
    real_part, imag_part = peramb
    upper = jnp.concatenate([real_part, -imag_part], axis=1)
    lower = jnp.concatenate([imag_part, real_part], axis=1)
    return jnp.concatenate([upper, lower], axis=0)


class Lane:
    def __init__(self, axis, depth):
        self.axis = axis
        self.depth = depth
        self.results = []

    def send(self, block, bit, *others):
        before = self.results[-self.depth :][: len(self.results) >= self.depth]
        block = after(block, *before, *others)
        result = lax.ppermute(block, self.axis, flip(lax.axis_size(self.axis), bit))
        self.results.append(result)
        return result


def after(value, *others):
    if not others:
        return value
    return lax.optimization_barrier((value, others))[0]


def per_device(elemental, perambulators, source_owner):
    owner = source_owner[0]
    row_count, col_count = lax.axis_size("row"), lax.axis_size("col")
    place = jnp.stack([lax.axis_index("row"), lax.axis_index("col")]).astype(jnp.int32)
    _, local_i, local_j, width = elemental.shape
    local_b, cols = width // row_count, width // col_count
    chosen = broadcast_rows(
        perambulators[0].reshape(2 * width, width), owner // col_count, owner % col_count
    )
    mixing = build_mixing(chosen.reshape(2, width, width))

    if cols % 128 or local_b % BLOCK or local_i % 16 or not is_power_of_two(row_count * col_count):
        mixing = mixing.reshape(2, width, 2, width)
        first = jnp.einsum("scrk,rijk->sijc", mixing, elemental, preferred_element_type=jnp.float32)
        first = lax.all_to_all(first.astype(jnp.bfloat16), "col", 3, 2, tiled=True)
        second = jnp.einsum("sbrj,rijc->sbic", mixing, first, preferred_element_type=jnp.float32)
        second = lax.all_to_all(second.astype(jnp.bfloat16), "row", 1, 2, tiled=True)
        return jnp.einsum("sari,rbic->sabc", mixing, second, preferred_element_type=jnp.float32)

    counts = [local_i * n // sum(COUNTS) for n in COUNTS[:-1]]
    counts.append(local_i - sum(counts))
    offsets = [sum(counts[:q]) for q in range(len(counts))]
    half = row_count // 2
    order = [half] + [t for n in range(1, half) for t in (n, half + n)]
    order[-2:] = order[:-3:-1]
    row_lane = Lane("row", DEPTH)
    last = len(counts) - 1
    tail = [BLOCK] * (local_b // BLOCK)
    chunks, tails = [], []

    def contract(q, *others):
        return contract_first(
            mixing, after(elemental, *others), offsets[q], counts[q], col_count
        )

    def send_first(block, *others):
        return lax.all_to_all(after(block, *others), "col", 0, 0, tiled=True)

    def send_second(part, waits):
        arrived = {0: part[0]}
        for n, t in enumerate(order):
            arrived[t] = row_lane.send(part[t], t, *waits.get(n, []))
        return [arrived[t] for t in range(row_count)]

    raw = lax.all_gather(elemental[:, : counts[0]], "col")
    following = contract(1)
    swapped = contract_gathered(mixing, raw, after(place, following))
    parts = contract_second(mixing, swapped, place, row_count, [local_b])
    swapped = send_first(following, swapped)
    for q in range(last):
        waits = {}
        if q + 2 <= last:
            following = contract(q + 2, parts[0][0])
            waits[FIRST] = [following]
        now = parts[0]
        parts = contract_second(
            mixing, swapped, place, row_count, tail if q + 1 == last else [local_b]
        )
        waits[SECOND] = [parts[0][0]]
        chunks.append(send_second(now, waits))
        if q + 2 <= last:
            held = [chunks[q][t] for t in order[:WAIT]]
            held += chunks[q - 1][1:] if q else []
            swapped = send_first(following, swapped, *held)
    for part in parts:
        tails.append(send_second(part, {}))
    result, index = None, 0
    for part, blocks in zip(tail, tails):
        for n in range(part // BLOCK):
            result = contract_third(
                mixing, chunks + [blocks], [index] * last + [n], place, offsets, index, local_b, result
            )
            index += 1
    return result.reshape(2, width, local_b, cols)


def solution(mesh):
    in_specs = (P(None, "row", "col", None), P(("row", "col"), None, None, None), P())
    out_specs = P(None, None, "row", "col")
    return jax.shard_map(
        per_device, mesh=mesh, in_specs=in_specs, out_specs=out_specs, check_vma=False
    )
```
